128 devices in a mesh: row: 8 (over x, core), col: 4 (over z), depth: 4 (over y).
Axes of the slice: x: 4, y: 4, z: 4, core: 2. Of those that a mesh axis runs over, the one named last changes fastest.
Arguments:
- packed: bfloat16 [36864, 2304], P(('row', 'col', 'depth')), may hold values from -6 to 6
- slot_blocks: int32 [36864], replicated, may hold values from 0 to 36863, as said below
- flip_bits: int32 [36864], P(('row', 'col', 'depth')), may hold values 0 or 1
- ladder_v: bfloat16 [36, 2304, 2048], P('depth', None, 'col'), may hold values from -0.01953125 to 0.01953125
Outputs:
- ladder: float32 [1024, 2048], P(('row', 'depth'), 'col')
The draws below stay inside these ranges and needn't reach their ends.
Inputs may be any that keep to these rules, and one draw needn't show every extreme that they name: `slot_blocks`: every block id appears exactly once. The device at mesh position (r, c, e) in row, col, depth order holds slots k from (r * col count + c) * depth count + e times 288 onward; it holds only blocks whose pair p has p mod col count equal to c, and exactly 9 blocks for each pair of indices (p // 128, t // 9).
All inputs are finite; a program needn't handle non-finite values. No bound on the sum of `flip_bits` on one device may be relied on, other than what follows from the above.
Results may differ from the reference program's by a relative error of at most 0.0003.
Values may be sent and summed in bfloat16 or wider, within the bound.
A program may use at most 192 MiB of HBM per device.

```python
import jax
import jax.numpy as jnp
import numpy as np

NV = 384
NB = 8
AB = 2048
PROW = 128
P_SIZE = 1024
TILE = 2304
NTILE = 36
N_ROW = 8
N_COL = 4
N_DEPTH = 4


def draw_slot_blocks(key, part):
    key = jax.random.fold_in(key, 11)
    first_key, second_key = jax.random.split(key)
    groups = N_ROW * N_DEPTH
    tiles_per = NTILE // N_DEPTH
    col_rows = PROW // N_COL
    within = col_rows * tiles_per
    per_peer = within // groups
    devices = N_ROW * N_COL * N_DEPTH
    keys_one = jax.random.split(first_key, N_COL * groups)
    orders = jax.vmap(lambda one: jax.random.permutation(one, within))(keys_one).reshape(N_COL, groups, within)
    pair_in_col = orders // tiles_per
    tile_in_group = orders % tiles_per
    col_index = jnp.arange(N_COL)[:, None, None]
    group_index = jnp.arange(groups)[None, :, None]
    pair_index = group_index // N_DEPTH * PROW + pair_in_col * N_COL + col_index
    tile_index = group_index % N_DEPTH * tiles_per + tile_in_group
    block_ids = pair_index * NTILE + tile_index
    block_ids = block_ids.reshape(N_COL, groups, N_ROW, N_DEPTH, per_peer)
    block_ids = jnp.transpose(block_ids, (2, 0, 3, 1, 4)).reshape(devices, groups * per_peer)
    keys_two = jax.random.split(second_key, devices)
    shuffled = jax.vmap(lambda one, line: jax.random.permutation(one, line))(keys_two, block_ids)
    return shuffled.reshape(-1).astype(jnp.int32)


def touch_ends(drawn, own_key, least, top_value):
    extent = drawn.shape
    index_at = [jax.random.randint(jax.random.fold_in(own_key, axis), (), 0, extent[axis]) for axis in range(len(extent))]
    drawn = drawn.at[tuple(index_at)].set(least)
    longest = extent.index(max(extent))
    index_at[longest] = (index_at[longest] + 1) % extent[longest]
    return drawn.at[tuple(index_at)].set(top_value)


def steps_of(rng, shape, shards, least, high):
    level, own = 1.0, jax.random.fold_in(rng, 6)
    for axis_at, blocks in shards:
        draws = jnp.exp(jax.random.uniform(jax.random.fold_in(own, axis_at), (blocks,), jnp.float32, least / len(shards), high / len(shards)))
        level = level * jnp.repeat(draws, shape[axis_at] // blocks).reshape([-1 if axis == axis_at else 1 for axis in range(len(shape))])
    return level


def normal_values(key, dims, scale, bound, cuts=(), kind=jnp.bfloat16):
    entries = jax.random.normal(key, dims, jnp.float32) * scale
    if len(cuts) > 0:
        entries = steps_of(key, dims, cuts, -0.22, 0.18) * entries
    return jnp.clip(entries, min=-bound, max=bound).astype(kind)


def setup_inputs(seed: int = 0) -> dict:
    arg_keys = jax.random.split(jax.random.key(seed), 5)
    packed = normal_values(arg_keys[0], (P_SIZE * NTILE, TILE), 1.0, 6.0, ((0, 128),))
    slot_blocks = draw_slot_blocks(jax.random.fold_in(arg_keys[4], 71), 0)
    flip_bits = touch_ends((jax.random.randint(arg_keys[2], (P_SIZE * NTILE,), 0, 2) < 1).astype(jnp.int32), jax.random.fold_in(arg_keys[2], 1), 0, 1)
    ladder_v = normal_values(arg_keys[3], (NTILE, TILE, AB), (NTILE * TILE) ** -0.5, 0.01953125, ((0, 4), (2, 4)))
    return {"packed": packed, "slot_blocks": slot_blocks, "flip_bits": flip_bits, "ladder_v": ladder_v}


def tile_weights(blocks):
    values = [0.5 if first == second else 1.0 for first in range(blocks) for second in range(first, blocks)]
    return jnp.asarray(np.array(values, dtype=np.float32))


def unpack(packed, flip_bits, tile_side):
    count = packed.shape[0]
    tiles = packed.reshape(count, tile_side, tile_side)
    turned = -jnp.swapaxes(tiles, 1, 2)
    chosen = jnp.where((flip_bits == 1)[:, None, None], turned, tiles)
    return chosen.reshape(count, tile_side * tile_side)


def reference(packed, slot_blocks, flip_bits, ladder_v):
    tile_side = NV // NB
    canonical = unpack(packed, flip_bits, tile_side)
    amplitudes = jnp.zeros((P_SIZE * NTILE, TILE), canonical.dtype).at[slot_blocks].set(canonical)
    amplitudes = amplitudes.reshape(P_SIZE, NTILE * TILE)
    weights = tile_weights(NB).astype(ladder_v.dtype)
    scaled_v = (ladder_v * weights[:, None, None]).reshape(NTILE * TILE, AB)
    return jnp.dot(amplitudes, scaled_v, preferred_element_type=jnp.float32)
```

```python
import jax
import jax.numpy as jnp
import numpy as np
from jax import lax
from jax.experimental import pallas as pl
from jax.experimental.pallas import tpu as pltpu
from jax.sharding import PartitionSpec as P

MESH = pl.DeviceIdType.MESH
SIDE = 48
TILE = SIDE * SIDE
HALF = TILE // 2
SLOTS = 288
X_ORDER = (0, 1, 3, 2)
DIAGONAL = (0, 8, 15, 21, 26, 30, 33, 35)
F32 = jnp.float32
BF16 = jnp.bfloat16


def turn_matrix():
    turn = np.zeros((TILE, TILE), np.float32)
    first, second = np.divmod(np.arange(TILE), SIDE)
    turn[second * SIDE + first, np.arange(TILE)] = -1.0
    return turn.astype(jnp.bfloat16)


def dot(a, b):
    return jnp.dot(a, b, preferred_element_type=F32)


def iota(shape, dim):
    return lax.broadcasted_iota(jnp.int32, shape, dim)


def split_ids(ids):
    pair = ((ids >> 2) * 7282) >> 16
    tile = ids - pair * 36
    part = (tile * 57) >> 9
    group = (pair >> 7) * 4 + part
    place = (tile - part * 9) * 32 + ((pair & 127) >> 2)
    return group, place


def kernel(
    packed_hbm, ids_ref, flip_ref, v_hbm, turn_hbm, out_ref,
    packed, turn, v, kept, turned, sbuf, rbuf, ybuf, dense, places, cbuf, yrec, mixed,
    load_sem, ssend, srecv, zsend, zrecv, fsend, frecv, ysend, yrecv,
):
    r, c, e = lax.axis_index("row"), lax.axis_index("col"), lax.axis_index("depth")
    x, k = r // 2, lax.rem(r, 2)
    here = k * 4 + e
    up, down = lax.rem(c + 1, 4), lax.rem(c + 3, 4)

    load_packed = pltpu.make_async_copy(packed_hbm, packed, load_sem.at[0])
    load_turn = pltpu.make_async_copy(turn_hbm, turn, load_sem.at[1])
    load_v = pltpu.make_async_copy(v_hbm, v, load_sem.at[2])
    load_packed.start()
    load_turn.start()

    barrier = pltpu.get_barrier_semaphore()
    for step in range(1, 32):
        other = lax.rem(r * 4 + e + step, 32)
        pl.semaphore_signal(
            barrier, inc=1, device_id=(other // 4, c, lax.rem(other, 4)), device_id_type=MESH
        )
    for z in (up, down):
        pl.semaphore_signal(barrier, inc=1, device_id=(r, z, e), device_id_type=MESH)

    before = jnp.where(iota((SLOTS, SLOTS), 0) < iota((SLOTS, SLOTS), 1), 1.0, 0.0).astype(BF16)
    flat = (r * 4 + c) * 4 + e
    group, _ = split_ids(ids_ref[pl.ds(flat, 1), :])
    member = jnp.where(iota((32, SLOTS), 0) == group, 1.0, 0.0)
    rank = jnp.sum(member * dot(member.astype(BF16), before), axis=0, keepdims=True)
    target = group * 16 + rank.astype(jnp.int32)
    flips = flip_ref[...] == 1

    load_packed.wait()
    load_turn.wait()

    def sort_stage(q):
        x_to = lax.rem(x + 4 - q, 4)
        hit = target - x_to * 128 == iota((128, SLOTS), 0)
        chosen = jnp.concatenate(
            [
                jnp.where(hit & jnp.logical_not(flips), 1.0, 0.0),
                jnp.where(hit & flips, 1.0, 0.0),
            ],
            axis=0,
        ).astype(BF16)

        def pick(n, _):
            cols = pl.ds(pl.multiple_of(n * 256, 256), 256)
            rows = dot(chosen, packed[:, cols])
            kept[:, cols] = rows[:128].astype(BF16)
            turned[:, cols] = rows[128:].astype(BF16)
            return 0

        lax.fori_loop(0, 9, pick, 0)

        def flip(n, _):
            cols = pl.ds(pl.multiple_of(n * 256, 256), 256)
            rows = dot(turned[...], turn[:, cols]) + kept[:, cols].astype(F32)
            sbuf[q, :, :, cols] = rows.astype(BF16).reshape(8, 16, 256)
            return 0

        lax.fori_loop(0, 9, flip, 0)

    def block_copy(q, step):
        x_to = lax.rem(x + 4 - q, 4)
        to = lax.rem(here + step, 8)
        return pltpu.make_async_remote_copy(
            src_ref=sbuf.at[q, to],
            dst_ref=rbuf.at[q, here],
            send_sem=ssend.at[q, step],
            recv_sem=srecv.at[q, step],
            device_id=(x_to * 2 + to // 4, c, lax.rem(to, 4)),
            device_id_type=MESH,
        )

    def steps(q):
        return range(1 if q == 0 else 0, 8)

    def send_stage(q):
        sort_stage(q)
        for step in steps(q):
            block_copy(q, step).start()
        if q == 0:
            rbuf[0, here] = sbuf[0, here]

    line, column = iota((144, 128), 0), iota((144, 128), 1)
    compact = []
    for h in range(2):
        inner = line - 72 * h
        wanted = (inner & 7) * 16 + (inner >> 3)
        hit = (inner >= 0) & (inner < 72) & (column == wanted)
        compact.append(jnp.where(hit, 1.0, 0.0).astype(BF16))

    def z_copy(q, j, direction):
        piece = 3 * q + j
        return pltpu.make_async_remote_copy(
            src_ref=ybuf.at[0, piece],
            dst_ref=ybuf.at[3 if direction == 0 else 1, piece],
            send_sem=zsend.at[direction, piece],
            recv_sem=zrecv.at[direction, piece],
            device_id=(r, up if direction == 0 else down, e),
            device_id_type=MESH,
        )

    def forward_copy(q, j):
        piece = 3 * q + j
        direction = (3 * X_ORDER.index(q) + j) % 2
        return pltpu.make_async_remote_copy(
            src_ref=ybuf.at[3 if direction == 0 else 1, piece],
            dst_ref=ybuf.at[2, piece],
            send_sem=fsend.at[piece],
            recv_sem=frecv.at[piece],
            device_id=(r, up if direction == 0 else down, e),
            device_id_type=MESH,
        )

    def gather_stage(q):
        for step in steps(q):
            block_copy(q, step).wait_recv()
        for n in range(3):
            low, high = n * 384, HALF + n * 384
            first = rbuf[q, :, :, low:low + 384].reshape(128, 384)
            second = rbuf[q, :, :, high:high + 384].reshape(128, 384)
            rows = dot(compact[0], first) + dot(compact[1], second)
            ybuf[0, 3 * q:3 * q + 3, :, low:low + 384] = rows.astype(BF16).reshape(3, 48, 384)
        for j in range(3):
            for direction in range(2):
                z_copy(q, j, direction).start()

    def forward_stage(q):
        for j in range(3):
            direction = (3 * X_ORDER.index(q) + j) % 2
            z_copy(q, j, direction).wait_recv()
            forward_copy(q, j).start()

    def find_places():
        groups, place = split_ids(ids_ref[...])
        mine = groups == r * 4 + e
        nth = dot(jnp.where(mine, 1.0, 0.0).astype(BF16), before)
        nth = jnp.where(mine, nth, -1.0)
        place = place.astype(F32)
        lanes = iota((128, 128), 1)
        table = jnp.full((128, 128), -1.0, F32)
        for n in range(9):
            found = jnp.sum(jnp.where(nth == n, place, 0.0), axis=1, keepdims=True)
            table = jnp.where(lanes == n, found, table)
        for x_at in range(4):
            for k_at in range(2):
                for c_at in range(4):
                    low = x_at * 32 + k_at * 16 + c_at * 4
                    places[c_at, x_at, k_at * 4:k_at * 4 + 4, :] = table[low:low + 4, :]

    scale_tile = iota((SLOTS, 1), 0) // 32 + e * 9
    diagonal = jnp.zeros((SLOTS, 1), jnp.bool_)
    for t in DIAGONAL:
        diagonal = diagonal | (scale_tile == t)
    scale = jnp.where(diagonal, 0.5, 1.0)

    def contract(slot):
        c_at = lax.rem(c + slot, 4)
        lines = []
        for q in range(4):
            one = places[c_at, lax.rem(x + q, 4)]
            half = [jnp.broadcast_to(one[:, n:n + 1], (8, 128)) for n in range(9)]
            lines += half + half
        wanted = jnp.concatenate(lines + [jnp.full((64, 128), -1.0, F32)], axis=0)
        wanted = jnp.transpose(wanted)[0:1, :576]
        hit = jnp.where(iota((SLOTS, 576), 0).astype(F32) == wanted, scale, 0.0)
        second = lax.rem(iota((1, 576), 1), 144) >= 72
        order = [
            jnp.where(second, 0.0, hit).astype(BF16),
            jnp.where(second, hit, 0.0).astype(BF16),
        ]
        for h in range(2):
            for n in range(3):
                rows = ybuf[slot, :, :, n * 384:(n + 1) * 384].reshape(576, 384)
                low = h * HALF + n * 384
                dense[:, low:low + 384] = dot(order[h], rows).astype(BF16)

        def add(t, total):
            rows = dense[pl.ds(pl.multiple_of(t * 32, 32), 32), :]
            return total + dot(rows, v[t])

        total = lax.fori_loop(0, 9, add, jnp.zeros((32, 512), F32))
        cbuf[c_at] = total.reshape(4, 8, 512)
        for step in range(1, 4):
            sum_copy(slot, step).start()

    def sum_copy(slot, step):
        c_at = lax.rem(c + slot, 4)
        to = lax.rem(e + step, 4)
        return pltpu.make_async_remote_copy(
            src_ref=cbuf.at[c_at, to],
            dst_ref=yrec.at[step - 1, c_at],
            send_sem=ysend.at[slot, step],
            recv_sem=yrecv.at[slot, step],
            device_id=(r, c, to),
            device_id_type=MESH,
        )

    pl.semaphore_wait(barrier, 33)
    send_stage(0)
    load_v.start()
    send_stage(1)
    gather_stage(0)
    send_stage(3)
    gather_stage(1)
    send_stage(2)
    forward_stage(0)
    find_places()
    gather_stage(3)
    forward_stage(1)
    gather_stage(2)
    load_v.wait()
    contract(0)
    forward_stage(3)
    forward_stage(2)
    for slot in (3, 1):
        direction = 0 if slot == 3 else 1
        for at, q in enumerate(X_ORDER):
            for j in range(3):
                if (3 * at + j) % 2 != direction:
                    z_copy(q, j, direction).wait_recv()
        contract(slot)
    for q in X_ORDER:
        for j in range(3):
            forward_copy(q, j).wait_recv()
    contract(2)

    for slot in range(4):
        for step in range(1, 4):
            sum_copy(slot, step).wait_recv()
    for c_at in range(4):
        total = cbuf[c_at, e]
        for step in range(1, 4):
            total = total + yrec[step - 1, c_at]
        for n in range(4):
            mixed[n, pl.ds(c_at, 8, stride=4), :] = total[:, n * 128:(n + 1) * 128]
    for n in range(4):
        out_ref[:, n * 128:(n + 1) * 128] = mixed[n]

    for q in range(4):
        for step in steps(q):
            block_copy(q, step).wait_send()
        for j in range(3):
            z_copy(q, j, 0).wait_send()
            z_copy(q, j, 1).wait_send()
            forward_copy(q, j).wait_send()
        for step in range(1, 4):
            sum_copy(q, step).wait_send()


def per_device(packed, slot_blocks, flip_bits, ladder_v):
    any_space = pl.BlockSpec(memory_space=pl.ANY)
    in_vmem = pl.BlockSpec(memory_space=pltpu.VMEM)
    dma = pltpu.SemaphoreType.DMA
    return pl.pallas_call(
        kernel,
        out_shape=jax.ShapeDtypeStruct((32, 512), F32),
        in_specs=[any_space, in_vmem, in_vmem, any_space, any_space],
        out_specs=in_vmem,
        scratch_shapes=[
            pltpu.VMEM((SLOTS, TILE), BF16),
            pltpu.VMEM((TILE, TILE), BF16),
            pltpu.VMEM((9, TILE, 512), BF16),
            pltpu.VMEM((128, TILE), BF16),
            pltpu.VMEM((128, TILE), BF16),
            pltpu.VMEM((4, 8, 16, TILE), BF16),
            pltpu.VMEM((4, 8, 16, TILE), BF16),
            pltpu.VMEM((4, 12, 48, HALF), BF16),
            pltpu.VMEM((SLOTS, TILE), BF16),
            pltpu.VMEM((4, 4, 8, 128), F32),
            pltpu.VMEM((4, 4, 8, 512), F32),
            pltpu.VMEM((3, 4, 8, 512), F32),
            pltpu.VMEM((4, 32, 128), F32),
            dma((3,)),
            dma((4, 8)),
            dma((4, 8)),
            dma((2, 12)),
            dma((2, 12)),
            dma((12,)),
            dma((12,)),
            dma((4, 4)),
            dma((4, 4)),
        ],
        compiler_params=pltpu.CompilerParams(
            collective_id=0, has_side_effects=True, vmem_limit_bytes=62 * 2**20
        ),
    )(
        packed,
        slot_blocks.reshape(128, SLOTS),
        flip_bits.reshape(1, SLOTS),
        ladder_v,
        jnp.asarray(turn_matrix()),
    )


def solution(mesh):
    in_specs = (
        P(("row", "col", "depth"), None),
        P(),
        P(("row", "col", "depth")),
        P("depth", None, "col"),
    )
    out_specs = P(("row", "depth"), "col")
    return jax.shard_map(
        per_device, mesh=mesh, in_specs=in_specs, out_specs=out_specs, check_vma=False
    )
```

```python
import jax
import jax.numpy as jnp
import numpy as np
from jax import lax
from jax.experimental import pallas as pl
from jax.experimental.pallas import tpu as pltpu
from jax.sharding import PartitionSpec as P


MESH = pl.DeviceIdType.MESH
TILE = 48 * 48
SLAB = 768
SLOTS = 288
X_ORDER = (0, 1, 3, 2)
DENSE_ORDER = (0, 3, 1, 2)
STEPS = ((0, 1), (0, 3), (1, 1), (1, 3), (0, 2), (1, 2), (1, 0))
DIAGONAL = (0, 8, 15, 21, 26, 30, 33, 35)
F32 = jnp.float32
BF16 = jnp.bfloat16


def part_matrix():
    a0, b1, b0 = np.meshgrid(np.arange(16), np.arange(3), np.arange(16), indexing="ij")
    out = np.zeros((SLAB, SLAB), np.float32)
    out[(a0 * 48 + b1 * 16 + b0).ravel(), (b1 * 256 + a0 * 16 + b0).ravel()] = 1.0
    return out.astype(jnp.bfloat16)


def dot(a, b):
    return jnp.dot(a, b, preferred_element_type=F32)


def iota(shape, dim):
    return lax.broadcasted_iota(jnp.int32, shape, dim)


def split_ids(ids):
    pair = ((ids >> 2) * 7282) >> 16
    tile = ids - pair * 36
    part = (tile * 57) >> 9
    group = (pair >> 7) * 4 + part
    place = (tile - part * 9) * 32 + ((pair & 127) >> 2)
    return group, place


def forward_direction(q, n):
    return (X_ORDER.index(q) + n) % 2


def kernel(
    packed_hbm, ids_hbm, flip_ref, v_hbm, part_hbm, out_ref,
    packed, ids_ref, part, v, nbuf, nrec, sbuf, xbuf, rbuf, ybuf, pmat, dense, table, places, cbuf, yrec, mixed,
    load_sem, v_sem, nsend, nrecv, xsend, xrecv, ssend, srecv, zsend, zrecv, fsend, frecv, ysend, yrecv,
):
    r, c, e = lax.axis_index("row"), lax.axis_index("col"), lax.axis_index("depth")
    x, k = r // 2, lax.rem(r, 2)
    here = k * 4 + e
    up, down = lax.rem(c + 1, 4), lax.rem(c + 3, 4)

    load_packed = pltpu.make_async_copy(packed_hbm, packed, load_sem.at[0])
    load_part = pltpu.make_async_copy(part_hbm, part, load_sem.at[1])
    load_ids = pltpu.make_async_copy(ids_hbm, ids_ref, load_sem.at[2])
    load_ids.start()
    load_packed.start()
    load_part.start()

    barrier = pltpu.get_barrier_semaphore()
    near = [(x * 2 + lax.rem(k + k_step, 2), c, lax.rem(e + e_step, 4)) for k_step, e_step in STEPS]
    near += [(lax.rem(x + step, 4) * 2 + k, c, e) for step in (1, 2, 3)]
    near += [(r, up, e), (r, down, e)]
    for device in near:
        pl.semaphore_signal(barrier, inc=1, device_id=device, device_id_type=MESH)

    def load_v(n, b):
        return pltpu.make_async_copy(v_hbm.at[:, n, :, b], v.at[n, :, b], v_sem.at[n, b])

    before = jnp.where(iota((SLOTS, SLOTS), 0) < iota((SLOTS, SLOTS), 1), 1.0, 0.0).astype(BF16)
    flat = (r * 4 + c) * 4 + e
    first = (flat * 9) // 4
    load_ids.wait()
    own = jnp.concatenate([ids_ref[pl.ds(first + i, 1), :] for i in range(3)], axis=1)
    own = pltpu.roll(own, lax.rem(384 - 32 * lax.rem(flat, 4), 384), 1)[:, :SLOTS]
    group, _ = split_ids(own)
    member = jnp.where(iota((32, SLOTS), 0) == group, 1.0, 0.0)
    rank = jnp.sum(member * dot(member.astype(BF16), before), axis=0, keepdims=True)
    target = group * 9 + rank.astype(jnp.int32)
    flips = flip_ref[...].reshape(1, SLOTS) == 1

    swap_in, swap_out = iota((256, 256), 0), iota((256, 256), 1)
    swap = (swap_in & 15) * 16 + (swap_in >> 4) == swap_out
    swap = jnp.where(swap, -1.0, 0.0).astype(BF16)

    def spread(a, rows):
        line, column = iota((8 * rows, 80), 0), iota((8 * rows, 80), 1)
        to, inner = line // rows, line % rows - 9 * a
        hit = (inner >= 0) & (inner < 9) & (column == to * 9 + inner)
        return jnp.where(hit, 1.0, 0.0).astype(BF16)

    spread_near = spread(0, 16)
    spread_far = [spread(a, 32) for a in range(3)]

    load_packed.wait()
    load_part.wait()

    def sort_stage(q):
        x_to = lax.rem(x + 4 - q, 4)
        line = iota((80, SLOTS), 0)
        hit = (target - x_to * 72 == line) & (line < 72)
        chosen = jnp.where(hit, 1.0, 0.0)
        turned = jnp.sum(jnp.where(flips, chosen, 0.0), axis=1, keepdims=True) > 0.5
        chosen = chosen.astype(BF16)
        parts = []
        for a in range(3):
            rows = dot(chosen, packed[:, a * SLAB:(a + 1) * SLAB]).astype(BF16)
            for b in range(3):
                parts.append(dot(rows, part[:, b * 256:(b + 1) * 256]))
        parts16 = [one.astype(BF16) for one in parts]

        def canon(a, b):
            return jnp.where(turned, dot(parts16[b * 3 + a], swap), parts[a * 3 + b]).astype(BF16)

        if q == 0:
            pl.semaphore_wait(barrier, len(near))
            for a in range(3):
                for b in range(3):
                    rows = dot(spread_near, canon(a, b)).astype(BF16)
                    nbuf[a, :, :, b * 256:(b + 1) * 256] = rows.reshape(8, 16, 256)
                send_near(a)
            return
        for b in range(3):
            total = dot(spread_far[0], canon(0, b))
            for a in range(1, 3):
                total = total + dot(spread_far[a], canon(a, b))
            sbuf[q - 1, :, :, b * 256:(b + 1) * 256] = total.astype(BF16).reshape(8, 32, 256)
        x_copy(q).start()

    def x_copy(q):
        return pltpu.make_async_remote_copy(
            src_ref=sbuf.at[q - 1],
            dst_ref=xbuf.at[q - 1],
            send_sem=xsend.at[q],
            recv_sem=xrecv.at[q],
            device_id=(lax.rem(x + 4 - q, 4) * 2 + k, c, e),
            device_id_type=MESH,
        )

    def near_place(step):
        k_step, e_step = STEPS[step]
        to_k, to_e = lax.rem(k + k_step, 2), lax.rem(e + e_step, 4)
        return to_k * 4 + to_e, (x * 2 + to_k, c, to_e)

    def near_copy(a, step):
        to, device = near_place(step)
        return pltpu.make_async_remote_copy(
            src_ref=nbuf.at[a, to],
            dst_ref=nrec.at[a, here],
            send_sem=nsend.at[a, step],
            recv_sem=nrecv.at[a, step],
            device_id=device,
            device_id_type=MESH,
        )

    def send_near(a):
        for step in range(7):
            near_copy(a, step).start()
        nrec[a, here] = nbuf[a, here]

    def block_copy(q, step):
        to, device = near_place(step)
        return pltpu.make_async_remote_copy(
            src_ref=xbuf.at[q - 1, to],
            dst_ref=rbuf.at[q - 1, here],
            send_sem=ssend.at[q, step],
            recv_sem=srecv.at[q, step],
            device_id=device,
            device_id_type=MESH,
        )

    def pass_blocks(q):
        x_copy(q).wait_recv()
        for step in range(7):
            block_copy(q, step).start()
        rbuf[q - 1, here] = xbuf[q - 1, here]

    def compact(n, h, rows):
        line, column = iota((144, 8 * rows), 0) - 72 * h, iota((144, 8 * rows), 1)
        wanted = (line & 7) * rows + n * 9 + (line >> 3)
        hit = (line >= 0) & (line < 72) & (column == wanted)
        return jnp.where(hit, 1.0, 0.0).astype(BF16)

    def z_copy(q, n, direction):
        at = X_ORDER.index(q)
        return pltpu.make_async_remote_copy(
            src_ref=ybuf.at[0, n, at],
            dst_ref=ybuf.at[3 if direction == 0 else 1, n, at],
            send_sem=zsend.at[direction, n, at],
            recv_sem=zrecv.at[direction, n, at],
            device_id=(r, up if direction == 0 else down, e),
            device_id_type=MESH,
        )

    def forward_copy(q, n):
        at = X_ORDER.index(q)
        direction = forward_direction(q, n)
        return pltpu.make_async_remote_copy(
            src_ref=ybuf.at[3 if direction == 0 else 1, n, at],
            dst_ref=ybuf.at[2, n, at],
            send_sem=fsend.at[n, at],
            recv_sem=frecv.at[n, at],
            device_id=(r, up if direction == 0 else down, e),
            device_id_type=MESH,
        )

    def send_piece(q, n, rows):
        ybuf[0, n, X_ORDER.index(q)] = rows.astype(BF16)
        for direction in range(2):
            z_copy(q, n, direction).start()

    def gather_near(n):
        for step in range(7):
            near_copy(n, step).wait_recv()
        low = nrec[n, :, :, :384].reshape(128, 384)
        high = nrec[n, :, :, 384:].reshape(128, 384)
        send_piece(0, n, dot(compact(0, 0, 16), low) + dot(compact(0, 1, 16), high))

    def gather_stage(q):
        for step in range(7):
            block_copy(q, step).wait_recv()
        low = rbuf[q - 1, :, :, :384].reshape(256, 384)
        high = rbuf[q - 1, :, :, 384:].reshape(256, 384)
        for n in range(3):
            send_piece(q, n, dot(compact(n, 0, 32), low) + dot(compact(n, 1, 32), high))

    def forward_stage(q, n):
        z_copy(q, n, forward_direction(q, n)).wait_recv()
        forward_copy(q, n).start()

    def wait_rest(slot, q, n):
        if slot == 2:
            forward_copy(q, n).wait_recv()
        elif slot != 0:
            direction = 0 if slot == 3 else 1
            if forward_direction(q, n) != direction:
                z_copy(q, n, direction).wait_recv()

    def find_places():
        ids = []
        for j in range(4):
            lines = [ids_ref[pl.ds((9 * j) // 4 + i, 32, stride=9), :] for i in range(3)]
            lines = jnp.concatenate(lines, axis=1)
            if j > 0:
                lines = pltpu.roll(lines, 384 - 32 * j, 1)
            ids.append(lines[:, :SLOTS])
        groups, place = split_ids(jnp.concatenate(ids, axis=0))
        mine = groups == r * 4 + e
        nth = dot(jnp.where(mine, 1.0, 0.0).astype(BF16), before)
        nth = jnp.where(mine, nth, -1.0)
        place = place.astype(F32)
        lanes = iota((128, 128), 1)
        found = jnp.full((128, 128), -1.0, F32)
        for n in range(9):
            value = jnp.sum(jnp.where(nth == n, place, 0.0), axis=1, keepdims=True)
            found = jnp.where(lanes == n, value, found)
        table[...] = found
        for j in range(4):
            for c_at in range(4):
                places[pl.ds(c_at * 32 + j, 8, stride=4), :] = table[pl.ds(j * 32 + c_at, 8, stride=4), :]

    scale_tile = iota((SLOTS, 1), 0) // 32 + e * 9
    diagonal = jnp.zeros((SLOTS, 1), jnp.bool_)
    for t in DIAGONAL:
        diagonal = diagonal | (scale_tile == t)
    scale = jnp.where(diagonal, 0.5, 1.0)

    none = jnp.full((8, 128), -1.0, F32)

    def find_order(slot):
        c_at = lax.rem(c + slot, 4)
        lines = [[], []]
        for q in X_ORDER:
            low = pl.multiple_of(c_at * 32 + lax.rem(x + q, 4) * 8, 8)
            one = places[pl.ds(low, 8), :]
            half = [jnp.broadcast_to(one[:, n:n + 1], (8, 128)) for n in range(9)]
            if q == X_ORDER[3]:
                lines = [line + [none, none] for line in lines]
            lines[0] += half + [none]
            lines[1] += [none] + half
        for h in range(2):
            wanted = jnp.transpose(jnp.concatenate(lines[h] + 6 * [none], axis=0))[0:1]
            hit = jnp.where(iota((SLOTS, 384), 0).astype(F32) == wanted, scale, 0.0)
            pmat[slot, h] = hit.astype(BF16)

    def place_blocks(slot, n, side):
        at = DENSE_ORDER.index(slot) * 32
        for h in range(2):
            if side == 0:
                blocks = [ybuf[slot, n, i, h * 64:h * 64 + 80, :] for i in range(3)]
                rows = dot(pmat[slot, h, :, :240], jnp.concatenate(blocks, axis=0))
            else:
                rows = dot(pmat[slot, h, :, 256:336], ybuf[slot, n, 3, h * 64:h * 64 + 80, :])
            rows = rows.reshape(9, 32, 384)
            cols = slice(h * 384, (h + 1) * 384)
            if side == 1:
                rows = rows + dense[n, :, at:at + 32, cols].astype(F32)
            dense[n, :, at:at + 32, cols] = rows.astype(BF16)

    def multiply(total, n, low, high):
        def add(t, total):
            return total + dot(dense[n, t, low:high, :], v[n, t].reshape(SLAB, 512))

        return lax.fori_loop(0, 9, add, total)

    def sum_copy(slot, step):
        c_at = lax.rem(c + slot, 4)
        to = lax.rem(e + step, 4)
        return pltpu.make_async_remote_copy(
            src_ref=cbuf.at[c_at, to],
            dst_ref=yrec.at[step - 1, c_at],
            send_sem=ysend.at[slot, step],
            recv_sem=yrecv.at[slot, step],
            device_id=(r, c, to),
            device_id_type=MESH,
        )

    def send_sums(slot, total):
        cbuf[lax.rem(c + slot, 4)] = total.reshape(4, 8, 512)
        for step in range(1, 4):
            sum_copy(slot, step).start()

    sort_stage(0)
    for n in range(3):
        for b in range(3):
            load_v(n, b).start()
    sort_stage(1)
    sort_stage(3)
    for n in range(3):
        gather_near(n)
    find_places()
    pass_blocks(1)
    sort_stage(2)
    for n in range(3):
        forward_stage(0, n)
    find_order(0)
    pass_blocks(3)
    gather_stage(1)
    for slot in (3, 1, 2):
        find_order(slot)
    gather_stage(3)
    for n in range(3):
        forward_stage(1, n)
    pass_blocks(2)
    for n in range(3):
        place_blocks(0, n, 0)
    gather_stage(2)
    for n in range(3):
        forward_stage(3, n)
    for n in range(3):
        for slot in (3, 1):
            for q in X_ORDER[:3]:
                wait_rest(slot, q, n)
            place_blocks(slot, n, 0)
        place_blocks(0, n, 1)
    for n in range(3):
        forward_stage(2, n)
    for n in range(3):
        for slot in (3, 1):
            wait_rest(slot, 2, n)
            place_blocks(slot, n, 1)
    total = jnp.zeros((96, 512), F32)
    for n in range(3):
        for b in range(3):
            load_v(n, b).wait()
        total = multiply(total, n, 0, 96)
    for at, slot in enumerate(DENSE_ORDER[:3]):
        send_sums(slot, total[at * 32:(at + 1) * 32])
    for n in range(3):
        for q in X_ORDER[:3]:
            wait_rest(2, q, n)
        place_blocks(2, n, 0)
    total = jnp.zeros((32, 512), F32)
    for n in range(3):
        wait_rest(2, 2, n)
        place_blocks(2, n, 1)
        total = multiply(total, n, 96, 128)
    send_sums(2, total)

    for slot in range(4):
        for step in range(1, 4):
            sum_copy(slot, step).wait_recv()
    for c_at in range(4):
        total = cbuf[c_at, e]
        for step in range(1, 4):
            total = total + yrec[step - 1, c_at]
        for n in range(4):
            mixed[n, pl.ds(c_at, 8, stride=4), :] = total[:, n * 128:(n + 1) * 128]
    for n in range(4):
        out_ref[:, n * 128:(n + 1) * 128] = mixed[n]

    for q in range(4):
        if q > 0:
            x_copy(q).wait_send()
            for step in range(7):
                block_copy(q, step).wait_send()
        else:
            for n in range(3):
                for step in range(7):
                    near_copy(n, step).wait_send()
        for n in range(3):
            z_copy(q, n, 0).wait_send()
            z_copy(q, n, 1).wait_send()
            forward_copy(q, n).wait_send()
        for step in range(1, 4):
            sum_copy(q, step).wait_send()


def per_device(packed, slot_blocks, flip_bits, ladder_v):
    any_space = pl.BlockSpec(memory_space=pl.ANY)
    in_vmem = pl.BlockSpec(memory_space=pltpu.VMEM)
    dma = pltpu.SemaphoreType.DMA
    return pl.pallas_call(
        kernel,
        out_shape=jax.ShapeDtypeStruct((32, 512), F32),
        in_specs=[any_space, any_space, in_vmem, any_space, any_space],
        out_specs=in_vmem,
        scratch_shapes=[
            pltpu.VMEM((SLOTS, TILE), BF16),
            pltpu.VMEM((SLOTS, 128), jnp.int32),
            pltpu.VMEM((SLAB, SLAB), BF16),
            pltpu.VMEM((3, 9, 3, 16, 16, 512), BF16),
            pltpu.VMEM((3, 8, 16, SLAB), BF16),
            pltpu.VMEM((3, 8, 16, SLAB), BF16),
            pltpu.VMEM((3, 8, 32, SLAB), BF16),
            pltpu.VMEM((3, 8, 32, SLAB), BF16),
            pltpu.VMEM((3, 8, 32, SLAB), BF16),
            pltpu.VMEM((4, 3, 4, 144, 384), BF16),
            pltpu.VMEM((4, 2, SLOTS, 384), BF16),
            pltpu.VMEM((3, 9, 128, SLAB), BF16),
            pltpu.VMEM((128, 128), F32),
            pltpu.VMEM((128, 128), F32),
            pltpu.VMEM((4, 4, 8, 512), F32),
            pltpu.VMEM((3, 4, 8, 512), F32),
            pltpu.VMEM((4, 32, 128), F32),
            dma((3,)),
            dma((3, 3)),
            dma((3, 7)),
            dma((3, 7)),
            dma((4,)),
            dma((4,)),
            dma((4, 7)),
            dma((4, 7)),
            dma((2, 3, 4)),
            dma((2, 3, 4)),
            dma((3, 4)),
            dma((3, 4)),
            dma((4, 4)),
            dma((4, 4)),
        ],
        compiler_params=pltpu.CompilerParams(
            collective_id=0, has_side_effects=True, vmem_limit_bytes=60 * 2**20
        ),
    )(
        packed,
        slot_blocks.reshape(SLOTS, 128),
        flip_bits,
        ladder_v.reshape(9, 3, 16, 3, 16, 512),
        jnp.asarray(part_matrix()),
    )


def solution(mesh):
    in_specs = (
        P(("row", "col", "depth"), None),
        P(),
        P(("row", "col", "depth")),
        P("depth", None, "col"),
    )
    out_specs = P(("row", "depth"), "col")
    return jax.shard_map(
        per_device, mesh=mesh, in_specs=in_specs, out_specs=out_specs, check_vma=False
    )
```

```python
import jax
import jax.numpy as jnp
import numpy as np
from jax import lax
from jax.experimental import pallas as pl
from jax.experimental.pallas import tpu as pltpu
from jax.sharding import PartitionSpec as P


MESH = pl.DeviceIdType.MESH
TILE = 48 * 48
SLAB = 768
SLOTS = 288
X_ORDER = (0, 1, 3, 2)
STEPS = ((0, 1), (0, 3), (1, 1), (1, 3), (0, 2), (1, 2), (1, 0))
DIAGONAL = (0, 8, 15, 21, 26, 30, 33, 35)
F32 = jnp.float32
BF16 = jnp.bfloat16


def part_matrix():
    a0, b1, b0 = np.meshgrid(np.arange(16), np.arange(3), np.arange(16), indexing="ij")
    out = np.zeros((SLAB, SLAB), np.float32)
    out[(a0 * 48 + b1 * 16 + b0).ravel(), (b1 * 256 + a0 * 16 + b0).ravel()] = 1.0
    return out.astype(jnp.bfloat16)


def dot(a, b):
    return jnp.dot(a, b, preferred_element_type=F32)


def iota(shape, dim):
    return lax.broadcasted_iota(jnp.int32, shape, dim)


def split_ids(ids):
    pair = ((ids >> 2) * 7282) >> 16
    tile = ids - pair * 36
    part = (tile * 57) >> 9
    group = (pair >> 7) * 4 + part
    place = (tile - part * 9) * 32 + ((pair & 127) >> 2)
    return group, place


def loop(count, body):
    def step(i, carry):
        body(i)
        return carry

    lax.fori_loop(0, count, step, 0)


def kernel(
    packed_hbm, ids_hbm, flip_ref, v_hbm, part_hbm, out_ref,
    packed, ids_ref, part, v, nbuf, nrec, sbuf, xbuf, rbuf, ybuf, pmat, dense, late, total, near_lines, lines_of, table, places, cbuf, yrec, mixed,
    load_sem, v_sem, nsend, nrecv, xsend, xrecv, ssend, srecv, zsend, zrecv, fsend, frecv, ysend, yrecv,
):
    r, c, e = lax.axis_index("row"), lax.axis_index("col"), lax.axis_index("depth")
    x, k = r // 2, lax.rem(r, 2)
    here = k * 4 + e
    up, down = lax.rem(c + 1, 4), lax.rem(c + 3, 4)

    load_packed = pltpu.make_async_copy(packed_hbm, packed, load_sem.at[0])
    load_part = pltpu.make_async_copy(part_hbm, part, load_sem.at[1])
    load_ids = pltpu.make_async_copy(ids_hbm, ids_ref, load_sem.at[2])
    load_ids.start()
    load_packed.start()
    load_part.start()

    barrier = pltpu.get_barrier_semaphore()
    near = [(x * 2 + lax.rem(k + k_step, 2), c, lax.rem(e + e_step, 4)) for k_step, e_step in STEPS]
    near += [(lax.rem(x + step, 4) * 2 + k, c, e) for step in (1, 2, 3)]
    near += [(r, up, e), (r, down, e)]
    for device in near:
        pl.semaphore_signal(barrier, inc=1, device_id=device, device_id_type=MESH)

    def load_v(n, b):
        return pltpu.make_async_copy(v_hbm.at[:, n, :, b], v.at[n, :, b], v_sem.at[n, b])

    before = jnp.where(iota((SLOTS, SLOTS), 0) < iota((SLOTS, SLOTS), 1), 1.0, 0.0).astype(BF16)
    flat = (r * 4 + c) * 4 + e
    first = (flat * 9) // 4
    load_ids.wait()
    own = jnp.concatenate([ids_ref[pl.ds(first + i, 1), :] for i in range(3)], axis=1)
    own = pltpu.roll(own, lax.rem(384 - 32 * lax.rem(flat, 4), 384), 1)[:, :SLOTS]
    group, _ = split_ids(own)
    member = jnp.where(iota((32, SLOTS), 0) == group, 1.0, 0.0)
    rank = jnp.sum(member * dot(member.astype(BF16), before), axis=0, keepdims=True)
    target = group * 9 + rank.astype(jnp.int32)
    flips = flip_ref[...].reshape(1, SLOTS) == 1

    swap_in, swap_out = iota((256, 256), 0), iota((256, 256), 1)
    swap = (swap_in & 15) * 16 + (swap_in >> 4) == swap_out
    swap = jnp.where(swap, -1.0, 0.0).astype(BF16)

    def spread(a, rows):
        line, column = iota((8 * rows, 80), 0), iota((8 * rows, 80), 1)
        to, inner = line // rows, line % rows - 9 * a
        hit = (inner >= 0) & (inner < 9) & (column == to * 9 + inner)
        return jnp.where(hit, 1.0, 0.0).astype(BF16)

    spread_near = spread(0, 16)
    spread_far = [spread(a, 32) for a in range(3)]

    load_packed.wait()
    load_part.wait()

    def sort_stage(q, is_near):
        x_to = lax.rem(x + 4 - q, 4)
        line = iota((80, SLOTS), 0)
        hit = (target - x_to * 72 == line) & (line < 72)
        chosen = jnp.where(hit, 1.0, 0.0)
        turned = jnp.sum(jnp.where(flips, chosen, 0.0), axis=1, keepdims=True) > 0.5
        chosen = chosen.astype(BF16)
        parts = []
        for a in range(3):
            rows = dot(chosen, packed[:, a * SLAB:(a + 1) * SLAB]).astype(BF16)
            for b in range(3):
                parts.append(dot(rows, part[:, b * 256:(b + 1) * 256]))
        parts16 = [one.astype(BF16) for one in parts]

        def canon(a, b):
            return jnp.where(turned, dot(parts16[b * 3 + a], swap), parts[a * 3 + b]).astype(BF16)

        if is_near:
            pl.semaphore_wait(barrier, len(near))
            for a in range(3):
                for b in range(3):
                    rows = dot(spread_near, canon(a, b)).astype(BF16)
                    nbuf[a, :, :, b * 256:(b + 1) * 256] = rows.reshape(8, 16, 256)
                if a == 0:
                    send_near(0)
            return
        for b in range(3):
            total = dot(spread_far[0], canon(0, b))
            for a in range(1, 3):
                total = total + dot(spread_far[a], canon(a, b))
            sbuf[q - 1, :, :, b * 256:(b + 1) * 256] = total.astype(BF16).reshape(8, 32, 256)

    def x_copy(q):
        return pltpu.make_async_remote_copy(
            src_ref=sbuf.at[q - 1],
            dst_ref=xbuf.at[q - 1],
            send_sem=xsend.at[q],
            recv_sem=xrecv.at[q],
            device_id=(lax.rem(x + 4 - q, 4) * 2 + k, c, e),
            device_id_type=MESH,
        )

    def near_place(step):
        k_step, e_step = STEPS[step]
        to_k, to_e = lax.rem(k + k_step, 2), lax.rem(e + e_step, 4)
        return to_k * 4 + to_e, (x * 2 + to_k, c, to_e)

    def near_copy(a, step):
        to, device = near_place(step)
        return pltpu.make_async_remote_copy(
            src_ref=nbuf.at[a, to],
            dst_ref=nrec.at[a, here],
            send_sem=nsend.at[a, step],
            recv_sem=nrecv.at[a, step],
            device_id=device,
            device_id_type=MESH,
        )

    def send_near(a):
        for step in range(7):
            near_copy(a, step).start()
        nrec[a, here] = nbuf[a, here]

    def block_copy(q, step):
        to, device = near_place(step)
        return pltpu.make_async_remote_copy(
            src_ref=xbuf.at[q - 1, to],
            dst_ref=rbuf.at[q - 1, here],
            send_sem=ssend.at[q, step],
            recv_sem=srecv.at[q, step],
            device_id=device,
            device_id_type=MESH,
        )

    def pass_blocks(q):
        x_copy(q).wait_recv()
        for step in range(7):
            block_copy(q, step).start()
        rbuf[q - 1, here] = xbuf[q - 1, here]

    def compact(n, h, rows):
        line, column = iota((144, 8 * rows), 0) - 72 * h, iota((144, 8 * rows), 1)
        wanted = (line & 7) * rows + n * 9 + (line >> 3)
        hit = (line >= 0) & (line < 72) & (column == wanted)
        return jnp.where(hit, 1.0, 0.0).astype(BF16)

    def z_copy(at, n, direction):
        return pltpu.make_async_remote_copy(
            src_ref=ybuf.at[0, n, at],
            dst_ref=ybuf.at[3 - 2 * direction, n, at],
            send_sem=zsend.at[direction, n, at],
            recv_sem=zrecv.at[direction, n, at],
            device_id=(r, lax.rem(c + 1 + 2 * direction, 4), e),
            device_id_type=MESH,
        )

    def forward_copy(at, n):
        direction = lax.rem(at + n, 2)
        return pltpu.make_async_remote_copy(
            src_ref=ybuf.at[3 - 2 * direction, n, at],
            dst_ref=ybuf.at[2, n, at],
            send_sem=fsend.at[n, at],
            recv_sem=frecv.at[n, at],
            device_id=(r, lax.rem(c + 1 + 2 * direction, 4), e),
            device_id_type=MESH,
        )

    def send_piece(at, n, rows):
        ybuf[0, n, at] = rows.astype(BF16)
        for direction in range(2):
            z_copy(at, n, direction).start()

    def gather_near(n):
        for step in range(7):
            near_copy(n, step).wait_recv()
        low = nrec[n, :, :, :384].reshape(128, 384)
        high = nrec[n, :, :, 384:].reshape(128, 384)
        send_piece(0, n, dot(near_lines[0], low) + dot(near_lines[1], high))

    def gather_stage(at):
        q = X_ORDER[at]
        for step in range(7):
            block_copy(q, step).wait_recv()

        def piece(n):
            low = rbuf[q - 1, :, :, :384].reshape(256, 384)
            high = rbuf[q - 1, :, :, 384:].reshape(256, 384)
            send_piece(at, n, dot(lines_of[n, 0], low) + dot(lines_of[n, 1], high))

        loop(3, piece)

    def forward_stage(at):
        def piece(n):
            z_copy(at, n, lax.rem(at + n, 2)).wait_recv()
            forward_copy(at, n).start()

        loop(3, piece)

    def wait_other(at, n):
        z_copy(at, n, lax.rem(at + n + 1, 2)).wait_recv()

    def find_places():
        ids = []
        for j in range(4):
            lines = [ids_ref[pl.ds((9 * j) // 4 + i, 32, stride=9), :] for i in range(3)]
            lines = jnp.concatenate(lines, axis=1)
            if j > 0:
                lines = pltpu.roll(lines, 384 - 32 * j, 1)
            ids.append(lines[:, :SLOTS])
        groups, place = split_ids(jnp.concatenate(ids, axis=0))
        mine = groups == r * 4 + e
        nth = dot(jnp.where(mine, 1.0, 0.0).astype(BF16), before)
        nth = jnp.where(mine, nth, -1.0)
        place = place.astype(F32)
        lanes = iota((128, 128), 1)
        found = jnp.full((128, 128), -1.0, F32)
        for n in range(9):
            value = jnp.sum(jnp.where(nth == n, place, 0.0), axis=1, keepdims=True)
            found = jnp.where(lanes == n, value, found)
        table[...] = found
        for j in range(4):
            for c_at in range(4):
                places[pl.ds(c_at * 32 + j, 8, stride=4), :] = table[pl.ds(j * 32 + c_at, 8, stride=4), :]

    scale_tile = iota((SLOTS, 1), 0) // 32 + e * 9
    diagonal = jnp.zeros((SLOTS, 1), jnp.bool_)
    for t in DIAGONAL:
        diagonal = diagonal | (scale_tile == t)
    scale = jnp.where(diagonal, 0.5, 1.0)

    none = jnp.full((8, 128), -1.0, F32)

    def find_order(slot):
        c_at = lax.rem(c + slot, 4)
        lines = [[], []]
        for at, q in enumerate(X_ORDER):
            low = pl.multiple_of(c_at * 32 + lax.rem(x + q, 4) * 8, 8)
            one = places[pl.ds(low, 8), :]
            half = [jnp.broadcast_to(one[:, n:n + 1], (8, 128)) for n in range(9)]
            if at == 2:
                lines = [line + 12 * [none] for line in lines]
            lines[0] += half + [none]
            lines[1] += [none] + half
        for h in range(2):
            wanted = jnp.transpose(jnp.concatenate(lines[h] + 12 * [none], axis=0))[0:1]
            hit = jnp.where(iota((SLOTS, 512), 0).astype(F32) == wanted, scale, 0.0)
            pmat[slot, h] = hit.astype(BF16)

    def place_blocks(slot, n, side, out, at, add=False):
        for h in range(2):
            blocks = [ybuf[slot, n, 2 * side + i, h * 64:h * 64 + 80, :] for i in range(2)]
            order = pmat[slot, h, :, side * 256:side * 256 + 160]
            rows = dot(order, jnp.concatenate(blocks, axis=0)).reshape(9, 32, 384)
            cols = slice(h * 384, (h + 1) * 384)
            if add:
                rows = rows + out[:, at, :, cols].astype(F32)
            out[:, at, :, cols] = rows.astype(BF16)

    def multiply(n, blocks, rows):
        def add(i):
            for half in range(2):
                cols = slice(half * 256, half * 256 + 256)
                some = [
                    dot(blocks[3 * i + t].reshape(rows, SLAB), v[n, 3 * i + t, :, :, :, cols].reshape(SLAB, 256))
                    for t in range(3)
                ]
                total[128 - rows:, cols] += some[0] + some[1] + some[2]

        loop(3, add)

    def multiply_early(n):
        for b in range(3):
            load_v(n, b).wait()
        multiply(n, dense.at[n], 128)

    def multiply_late(n):
        wait_other(2, n)
        wait_other(3, n)
        loop(2, lambda i: place_blocks(1 + 2 * i, n, 1, late, 2 * i))
        forward_copy(2, n).wait_recv()
        forward_copy(3, n).wait_recv()
        place_blocks(2, n, 1, late, 1)

        multiply(n, late, 96)

    def sum_copy(slot, step):
        c_at = lax.rem(c + slot, 4)
        to = lax.rem(e + step, 4)
        return pltpu.make_async_remote_copy(
            src_ref=cbuf.at[c_at, to],
            dst_ref=yrec.at[step - 1, c_at],
            send_sem=ysend.at[slot, step],
            recv_sem=yrecv.at[slot, step],
            device_id=(r, c, to),
            device_id_type=MESH,
        )

    def send_sums(slot):
        cbuf[lax.rem(c + slot, 4)] = total[slot * 32:(slot + 1) * 32].reshape(4, 8, 512)
        for step in range(1, 4):
            sum_copy(slot, step).start()

    sort_stage(0, True)
    for n in range(3):
        for b in range(3):
            load_v(n, b).start()

    near_lines[0] = compact(0, 0, 16)
    near_lines[1] = compact(0, 1, 16)
    for n in range(3):
        for h in range(2):
            lines_of[n, h] = compact(n, h, 32)

    def far_stage(i):
        q = 1 + 2 * i - 3 * (i // 2)

        @pl.when(i == 2)
        def _():
            loop(3, gather_near)

        sort_stage(q, False)

        @pl.when(i < 2)
        def _():
            x_copy(q).start()
            for step in range(7):
                near_copy(i, step).wait_send()
            send_near(i + 1)

    loop(3, far_stage)
    find_places()
    pass_blocks(1)
    x_copy(2).start()
    loop(4, find_order)
    forward_stage(0)
    pass_blocks(3)
    gather_stage(1)
    gather_stage(2)
    pass_blocks(2)
    forward_stage(1)
    loop(3, lambda n: place_blocks(0, n, 0, dense.at[n], 0))
    gather_stage(3)
    loop(3, lambda n: place_blocks(0, n, 1, dense.at[n], 0, add=True))
    for n in range(3):
        wait_other(0, n)
        wait_other(1, n)
    loop(6, lambda i: place_blocks(1 + 2 * (i // 3), lax.rem(i, 3), 0, dense.at[lax.rem(i, 3)], 1 + 2 * (i // 3)))
    total[...] = jnp.zeros((128, 512), F32)
    forward_stage(2)
    for n in range(3):
        forward_copy(0, n).wait_recv()
        forward_copy(1, n).wait_recv()
    loop(3, lambda n: place_blocks(2, n, 0, dense.at[n], 2))
    loop(3, multiply_early)
    send_sums(0)
    forward_stage(3)
    loop(3, multiply_late)
    for slot in range(1, 4):
        send_sums(slot)

    for slot in range(4):
        for step in range(1, 4):
            sum_copy(slot, step).wait_recv()
    for c_at in range(4):
        rows = cbuf[c_at, e]
        for step in range(1, 4):
            rows = rows + yrec[step - 1, c_at]
        for n in range(4):
            mixed[n, pl.ds(c_at, 8, stride=4), :] = rows[:, n * 128:(n + 1) * 128]
    for n in range(4):
        out_ref[:, n * 128:(n + 1) * 128] = mixed[n]

    for q in range(4):
        if q > 0:
            x_copy(q).wait_send()
            for step in range(7):
                block_copy(q, step).wait_send()
        else:
            for step in range(7):
                near_copy(2, step).wait_send()
        for n in range(3):
            z_copy(q, n, 0).wait_send()
            z_copy(q, n, 1).wait_send()
            forward_copy(q, n).wait_send()
        for step in range(1, 4):
            sum_copy(q, step).wait_send()


def per_device(packed, slot_blocks, flip_bits, ladder_v):
    any_space = pl.BlockSpec(memory_space=pl.ANY)
    in_vmem = pl.BlockSpec(memory_space=pltpu.VMEM)
    dma = pltpu.SemaphoreType.DMA
    return pl.pallas_call(
        kernel,
        out_shape=jax.ShapeDtypeStruct((32, 512), F32),
        in_specs=[any_space, any_space, in_vmem, any_space, any_space],
        out_specs=in_vmem,
        scratch_shapes=[
            pltpu.VMEM((SLOTS, TILE), BF16),
            pltpu.VMEM((SLOTS, 128), jnp.int32),
            pltpu.VMEM((SLAB, SLAB), BF16),
            pltpu.VMEM((3, 9, 3, 16, 16, 512), BF16),
            pltpu.VMEM((3, 8, 16, SLAB), BF16),
            pltpu.VMEM((3, 8, 16, SLAB), BF16),
            pltpu.VMEM((3, 8, 32, SLAB), BF16),
            pltpu.VMEM((3, 8, 32, SLAB), BF16),
            pltpu.VMEM((3, 8, 32, SLAB), BF16),
            pltpu.VMEM((4, 3, 4, 144, 384), BF16),
            pltpu.VMEM((4, 2, SLOTS, 512), BF16),
            pltpu.VMEM((3, 9, 4, 32, SLAB), BF16),
            pltpu.VMEM((9, 3, 32, SLAB), BF16),
            pltpu.VMEM((128, 512), F32),
            pltpu.VMEM((2, 144, 128), BF16),
            pltpu.VMEM((3, 2, 144, 256), BF16),
            pltpu.VMEM((128, 128), F32),
            pltpu.VMEM((128, 128), F32),
            pltpu.VMEM((4, 4, 8, 512), F32),
            pltpu.VMEM((3, 4, 8, 512), F32),
            pltpu.VMEM((4, 32, 128), F32),
            dma((3,)),
            dma((3, 3)),
            dma((3, 7)),
            dma((3, 7)),
            dma((4,)),
            dma((4,)),
            dma((4, 7)),
            dma((4, 7)),
            dma((2, 3, 4)),
            dma((2, 3, 4)),
            dma((3, 4)),
            dma((3, 4)),
            dma((4, 4)),
            dma((4, 4)),
        ],
        compiler_params=pltpu.CompilerParams(
            collective_id=0, has_side_effects=True, vmem_limit_bytes=60 * 2**20
        ),
    )(
        packed,
        slot_blocks.reshape(SLOTS, 128),
        flip_bits,
        ladder_v.reshape(9, 3, 16, 3, 16, 512),
        jnp.asarray(part_matrix()),
    )


def solution(mesh):
    in_specs = (
        P(("row", "col", "depth"), None),
        P(),
        P(("row", "col", "depth")),
        P("depth", None, "col"),
    )
    out_specs = P(("row", "depth"), "col")
    return jax.shard_map(
        per_device, mesh=mesh, in_specs=in_specs, out_specs=out_specs, check_vma=False
    )
```

```python
import jax
import jax.numpy as jnp
import numpy as np
from jax import lax
from jax.experimental import pallas as pl
from jax.experimental.pallas import tpu as pltpu
from jax.sharding import PartitionSpec as P


MESH = pl.DeviceIdType.MESH
TILE = 48 * 48
SLAB = 768
SLOTS = 288
X_ORDER = (0, 1, 3, 2)
STEPS = ((0, 1), (0, 3), (1, 1), (1, 3), (0, 2), (1, 2), (1, 0))
DIAGONAL = (0, 8, 15, 21, 26, 30, 33, 35)
F32 = jnp.float32
BF16 = jnp.bfloat16


def part_matrix():
    a0, b1, b0 = np.meshgrid(np.arange(16), np.arange(3), np.arange(16), indexing="ij")
    out = np.zeros((SLAB, SLAB), np.float32)
    out[(a0 * 48 + b1 * 16 + b0).ravel(), (b1 * 256 + a0 * 16 + b0).ravel()] = 1.0
    return out.astype(jnp.bfloat16)


def dot(a, b):
    return jnp.dot(a, b, preferred_element_type=F32)


def iota(shape, dim):
    return lax.broadcasted_iota(jnp.int32, shape, dim)


def split_ids(ids):
    pair = ((ids >> 2) * 7282) >> 16
    tile = ids - pair * 36
    part = (tile * 57) >> 9
    group = (pair >> 7) * 4 + part
    place = (tile - part * 9) * 32 + ((pair & 127) >> 2)
    return group, place


def loop(count, body):
    def step(i, carry):
        body(i)
        return carry

    lax.fori_loop(0, count, step, 0)


def kernel(
    packed_hbm, ids_hbm, flip_ref, v_hbm, part_hbm, out_ref,
    packed, ids_ref, part, v, nbuf, nrec, sbuf, xbuf, rbuf, ybuf, pmat, dense, late, total, near_lines, lines_of, table, places, cbuf, yrec, mixed,
    load_sem, v_sem, nsend, nrecv, xsend, xrecv, ssend, srecv, zsend, zrecv, fsend, frecv, ysend, yrecv,
):
    r, c, e = lax.axis_index("row"), lax.axis_index("col"), lax.axis_index("depth")
    x, k = r // 2, lax.rem(r, 2)
    here = k * 4 + e
    up, down = lax.rem(c + 1, 4), lax.rem(c + 3, 4)

    load_packed = pltpu.make_async_copy(packed_hbm, packed, load_sem.at[0])
    load_part = pltpu.make_async_copy(part_hbm, part, load_sem.at[1])
    load_ids = pltpu.make_async_copy(ids_hbm, ids_ref, load_sem.at[2])
    load_ids.start()
    load_packed.start()
    load_part.start()

    barrier = pltpu.get_barrier_semaphore()
    near = [(x * 2 + lax.rem(k + k_step, 2), c, lax.rem(e + e_step, 4)) for k_step, e_step in STEPS]
    near += [(lax.rem(x + step, 4) * 2 + k, c, e) for step in (1, 2, 3)]
    near += [(r, up, e), (r, down, e)]
    for device in near:
        pl.semaphore_signal(barrier, inc=1, device_id=device, device_id_type=MESH)

    def load_v(n, b):
        return pltpu.make_async_copy(v_hbm.at[:, n, :, b], v.at[n, :, b], v_sem.at[n, b])

    before = jnp.where(iota((SLOTS, SLOTS), 0) < iota((SLOTS, SLOTS), 1), 1.0, 0.0).astype(BF16)
    flat = (r * 4 + c) * 4 + e
    first = (flat * 9) // 4
    load_ids.wait()
    own = jnp.concatenate([ids_ref[pl.ds(first + i, 1), :] for i in range(3)], axis=1)
    own = pltpu.roll(own, lax.rem(384 - 32 * lax.rem(flat, 4), 384), 1)[:, :SLOTS]
    group, _ = split_ids(own)
    member = jnp.where(iota((32, SLOTS), 0) == group, 1.0, 0.0)
    rank = jnp.sum(member * dot(member.astype(BF16), before), axis=0, keepdims=True)
    target = group * 9 + rank.astype(jnp.int32)
    flips = flip_ref[...].reshape(1, SLOTS) == 1

    swap_in, swap_out = iota((256, 256), 0), iota((256, 256), 1)
    swap = (swap_in & 15) * 16 + (swap_in >> 4) == swap_out
    swap = jnp.where(swap, -1.0, 0.0).astype(BF16)

    def spread(a, rows):
        line, column = iota((8 * rows, 80), 0), iota((8 * rows, 80), 1)
        to, inner = line // rows, line % rows - 9 * a
        hit = (inner >= 0) & (inner < 9) & (column == to * 9 + inner)
        return jnp.where(hit, 1.0, 0.0).astype(BF16)

    spread_near = spread(0, 16)
    spread_far = [spread(a, 32) for a in range(3)]

    load_packed.wait()
    load_part.wait()

    def sort_stage(q, is_near):
        x_to = lax.rem(x + 4 - q, 4)
        line = iota((80, SLOTS), 0)
        hit = (target - x_to * 72 == line) & (line < 72)
        chosen = jnp.where(hit, 1.0, 0.0)
        turned = jnp.sum(jnp.where(flips, chosen, 0.0), axis=1, keepdims=True) > 0.5
        chosen = chosen.astype(BF16)
        parts = []
        for a in range(3):
            rows = dot(chosen, packed[:, a * SLAB:(a + 1) * SLAB]).astype(BF16)
            for b in range(3):
                parts.append(dot(rows, part[:, b * 256:(b + 1) * 256]))
        parts16 = [one.astype(BF16) for one in parts]

        def canon(a, b):
            return jnp.where(turned, dot(parts16[b * 3 + a], swap), parts[a * 3 + b]).astype(BF16)

        if is_near:
            pl.semaphore_wait(barrier, len(near))
            for a in range(3):
                for b in range(3):
                    rows = dot(spread_near, canon(a, b)).astype(BF16)
                    nbuf[a, :, :, b * 256:(b + 1) * 256] = rows.reshape(8, 16, 256)
                if a == 0:
                    send_near(0)
            return
        for b in range(3):
            total = dot(spread_far[0], canon(0, b))
            for a in range(1, 3):
                total = total + dot(spread_far[a], canon(a, b))
            sbuf[q - 1, :, :, b * 256:(b + 1) * 256] = total.astype(BF16).reshape(8, 32, 256)

    def x_copy(q):
        return pltpu.make_async_remote_copy(
            src_ref=sbuf.at[q - 1],
            dst_ref=xbuf.at[q - 1],
            send_sem=xsend.at[q],
            recv_sem=xrecv.at[q],
            device_id=(lax.rem(x + 4 - q, 4) * 2 + k, c, e),
            device_id_type=MESH,
        )

    def near_place(step):
        k_step, e_step = STEPS[step]
        to_k, to_e = lax.rem(k + k_step, 2), lax.rem(e + e_step, 4)
        return to_k * 4 + to_e, (x * 2 + to_k, c, to_e)

    def near_copy(a, step):
        to, device = near_place(step)
        return pltpu.make_async_remote_copy(
            src_ref=nbuf.at[a, to],
            dst_ref=nrec.at[a, here],
            send_sem=nsend.at[a, step],
            recv_sem=nrecv.at[a, step],
            device_id=device,
            device_id_type=MESH,
        )

    def send_near(a):
        for step in range(7):
            near_copy(a, step).start()
        nrec[a, here] = nbuf[a, here]

    def block_copy(q, step):
        to, device = near_place(step)
        return pltpu.make_async_remote_copy(
            src_ref=xbuf.at[q - 1, to],
            dst_ref=rbuf.at[q - 1, here],
            send_sem=ssend.at[q, step],
            recv_sem=srecv.at[q, step],
            device_id=device,
            device_id_type=MESH,
        )

    def pass_blocks(q):
        x_copy(q).wait_recv()
        for step in range(7):
            block_copy(q, step).start()
        rbuf[q - 1, here] = xbuf[q - 1, here]

    def compact(n, h, rows):
        line, column = iota((144, 8 * rows), 0) - 72 * h, iota((144, 8 * rows), 1)
        wanted = (line & 7) * rows + n * 9 + (line >> 3)
        hit = (line >= 0) & (line < 72) & (column == wanted)
        return jnp.where(hit, 1.0, 0.0).astype(BF16)

    def z_copy(at, n, direction):
        return pltpu.make_async_remote_copy(
            src_ref=ybuf.at[0, n, at],
            dst_ref=ybuf.at[3 - 2 * direction, n, at],
            send_sem=zsend.at[direction, n, at],
            recv_sem=zrecv.at[direction, n, at],
            device_id=(r, lax.rem(c + 1 + 2 * direction, 4), e),
            device_id_type=MESH,
        )

    def forward_copy(at, n):
        direction = lax.rem(at + n, 2)
        return pltpu.make_async_remote_copy(
            src_ref=ybuf.at[3 - 2 * direction, n, at],
            dst_ref=ybuf.at[2, n, at],
            send_sem=fsend.at[n, at],
            recv_sem=frecv.at[n, at],
            device_id=(r, lax.rem(c + 1 + 2 * direction, 4), e),
            device_id_type=MESH,
        )

    def send_piece(at, n, rows):
        ybuf[0, n, at] = rows.astype(BF16)
        for direction in range(2):
            z_copy(at, n, direction).start()

    def gather_near(n):
        for step in range(7):
            near_copy(n, step).wait_recv()
        low = nrec[n, :, :, :384].reshape(128, 384)
        high = nrec[n, :, :, 384:].reshape(128, 384)
        send_piece(0, n, dot(near_lines[0], low) + dot(near_lines[1], high))

    def gather_stage(at):
        q = X_ORDER[at]
        for step in range(7):
            block_copy(q, step).wait_recv()

        def piece(n):
            low = rbuf[q - 1, :, :, :384].reshape(256, 384)
            high = rbuf[q - 1, :, :, 384:].reshape(256, 384)
            send_piece(at, n, dot(lines_of[n, 0], low) + dot(lines_of[n, 1], high))

        loop(3, piece)

    def forward_stage(at):
        def piece(n):
            z_copy(at, n, lax.rem(at + n, 2)).wait_recv()
            forward_copy(at, n).start()

        loop(3, piece)

    def wait_other(at, n):
        z_copy(at, n, lax.rem(at + n + 1, 2)).wait_recv()

    def find_places():
        ids = []
        for j in range(4):
            lines = [ids_ref[pl.ds((9 * j) // 4 + i, 32, stride=9), :] for i in range(3)]
            lines = jnp.concatenate(lines, axis=1)
            if j > 0:
                lines = pltpu.roll(lines, 384 - 32 * j, 1)
            ids.append(lines[:, :SLOTS])
        groups, place = split_ids(jnp.concatenate(ids, axis=0))
        mine = groups == r * 4 + e
        nth = dot(jnp.where(mine, 1.0, 0.0).astype(BF16), before)
        nth = jnp.where(mine, nth, -1.0)
        place = place.astype(F32)
        lanes = iota((128, 128), 1)
        found = jnp.full((128, 128), -1.0, F32)
        for n in range(9):
            value = jnp.sum(jnp.where(nth == n, place, 0.0), axis=1, keepdims=True)
            found = jnp.where(lanes == n, value, found)
        table[...] = found
        for j in range(4):
            for c_at in range(4):
                places[pl.ds(c_at * 32 + j, 8, stride=4), :] = table[pl.ds(j * 32 + c_at, 8, stride=4), :]

    scale_tile = iota((SLOTS, 1), 0) // 32 + e * 9
    diagonal = jnp.zeros((SLOTS, 1), jnp.bool_)
    for t in DIAGONAL:
        diagonal = diagonal | (scale_tile == t)
    scale = jnp.where(diagonal, 0.5, 1.0)

    none = jnp.full((8, 128), -1.0, F32)

    def find_order(slot):
        c_at = lax.rem(c + slot, 4)
        lines = [[], []]
        for at, q in enumerate(X_ORDER):
            low = pl.multiple_of(c_at * 32 + lax.rem(x + q, 4) * 8, 8)
            one = places[pl.ds(low, 8), :]
            half = [jnp.broadcast_to(one[:, n:n + 1], (8, 128)) for n in range(9)]
            if at == 2:
                lines = [line + 12 * [none] for line in lines]
            lines[0] += half + [none]
            lines[1] += [none] + half
        for h in range(2):
            wanted = jnp.transpose(jnp.concatenate(lines[h] + 12 * [none], axis=0))[0:1]
            hit = jnp.where(iota((SLOTS, 512), 0).astype(F32) == wanted, scale, 0.0)
            pmat[slot, h] = hit.astype(BF16)

    def place_blocks(slot, n, side, out, at, add=False):
        for h in range(2):
            blocks = [ybuf[slot, n, 2 * side + i, h * 64:h * 64 + 80, :] for i in range(2)]
            order = pmat[slot, h, :, side * 256:side * 256 + 160]
            rows = dot(order, jnp.concatenate(blocks, axis=0)).reshape(9, 32, 384)
            cols = slice(h * 384, (h + 1) * 384)
            if add:
                rows = rows + out[:, at, :, cols].astype(F32)
            out[:, at, :, cols] = rows.astype(BF16)

    def multiply(n, blocks, rows):
        for half in range(2):
            cols = slice(half * 256, half * 256 + 256)
            some = [
                dot(blocks[t].reshape(rows, SLAB), v[n, t, :, :, :, cols].reshape(SLAB, 256))
                for t in range(9)
            ]
            total[128 - rows:, cols] += sum(some[1:], some[0])

    def multiply_early(n):
        for b in range(3):
            load_v(n, b).wait()
        multiply(n, dense.at[n], 128)

    def multiply_late(n):
        wait_other(2, n)
        wait_other(3, n)
        place_blocks(1, n, 1, late, 0)
        place_blocks(3, n, 1, late, 2)
        forward_copy(2, n).wait_recv()
        forward_copy(3, n).wait_recv()
        place_blocks(2, n, 1, late, 1)

        multiply(n, late, 96)

    def sum_copy(slot, step):
        c_at = lax.rem(c + slot, 4)
        to = lax.rem(e + step, 4)
        return pltpu.make_async_remote_copy(
            src_ref=cbuf.at[c_at, to],
            dst_ref=yrec.at[step - 1, c_at],
            send_sem=ysend.at[slot, step],
            recv_sem=yrecv.at[slot, step],
            device_id=(r, c, to),
            device_id_type=MESH,
        )

    def send_sums(slot):
        cbuf[lax.rem(c + slot, 4)] = total[slot * 32:(slot + 1) * 32].reshape(4, 8, 512)
        for step in range(1, 4):
            sum_copy(slot, step).start()

    sort_stage(0, True)
    for n in range(3):
        for b in range(3):
            load_v(n, b).start()

    near_lines[0] = compact(0, 0, 16)
    near_lines[1] = compact(0, 1, 16)
    for n in range(3):
        for h in range(2):
            lines_of[n, h] = compact(n, h, 32)

    def far_stage(i):
        q = 1 + 2 * i - 3 * (i // 2)

        @pl.when(i == 2)
        def _():
            loop(3, gather_near)

        sort_stage(q, False)

        @pl.when(i < 2)
        def _():
            x_copy(q).start()
            for step in range(7):
                near_copy(i, step).wait_send()
            send_near(i + 1)

    loop(3, far_stage)
    find_places()
    pass_blocks(1)
    x_copy(2).start()
    loop(4, find_order)
    forward_stage(0)
    pass_blocks(3)
    gather_stage(1)
    gather_stage(2)
    pass_blocks(2)
    forward_stage(1)
    loop(3, lambda n: place_blocks(0, n, 0, dense.at[n], 0))
    for n in range(3):
        wait_other(0, n)
        wait_other(1, n)
    loop(6, lambda i: place_blocks(1 + 2 * (i // 3), lax.rem(i, 3), 0, dense.at[lax.rem(i, 3)], 1 + 2 * (i // 3)))
    total[...] = jnp.zeros((128, 512), F32)
    forward_stage(2)
    gather_stage(3)
    loop(3, lambda n: place_blocks(0, n, 1, dense.at[n], 0, add=True))
    for n in range(3):
        forward_copy(0, n).wait_recv()
        forward_copy(1, n).wait_recv()
    loop(3, lambda n: place_blocks(2, n, 0, dense.at[n], 2))
    loop(3, multiply_early)
    send_sums(0)
    forward_stage(3)
    loop(3, multiply_late)
    for slot in range(1, 4):
        send_sums(slot)

    for slot in range(4):
        for step in range(1, 4):
            sum_copy(slot, step).wait_recv()
    for c_at in range(4):
        rows = cbuf[c_at, e]
        for step in range(1, 4):
            rows = rows + yrec[step - 1, c_at]
        for n in range(4):
            mixed[n, pl.ds(c_at, 8, stride=4), :] = rows[:, n * 128:(n + 1) * 128]
    for n in range(4):
        out_ref[:, n * 128:(n + 1) * 128] = mixed[n]

    for q in range(4):
        if q > 0:
            x_copy(q).wait_send()
            for step in range(7):
                block_copy(q, step).wait_send()
        else:
            for step in range(7):
                near_copy(2, step).wait_send()
        for n in range(3):
            z_copy(q, n, 0).wait_send()
            z_copy(q, n, 1).wait_send()
            forward_copy(q, n).wait_send()
        for step in range(1, 4):
            sum_copy(q, step).wait_send()


def per_device(packed, slot_blocks, flip_bits, ladder_v):
    any_space = pl.BlockSpec(memory_space=pl.ANY)
    in_vmem = pl.BlockSpec(memory_space=pltpu.VMEM)
    dma = pltpu.SemaphoreType.DMA
    return pl.pallas_call(
        kernel,
        out_shape=jax.ShapeDtypeStruct((32, 512), F32),
        in_specs=[any_space, any_space, in_vmem, any_space, any_space],
        out_specs=in_vmem,
        scratch_shapes=[
            pltpu.VMEM((SLOTS, TILE), BF16),
            pltpu.VMEM((SLOTS, 128), jnp.int32),
            pltpu.VMEM((SLAB, SLAB), BF16),
            pltpu.VMEM((3, 9, 3, 16, 16, 512), BF16),
            pltpu.VMEM((3, 8, 16, SLAB), BF16),
            pltpu.VMEM((3, 8, 16, SLAB), BF16),
            pltpu.VMEM((3, 8, 32, SLAB), BF16),
            pltpu.VMEM((3, 8, 32, SLAB), BF16),
            pltpu.VMEM((3, 8, 32, SLAB), BF16),
            pltpu.VMEM((4, 3, 4, 144, 384), BF16),
            pltpu.VMEM((4, 2, SLOTS, 512), BF16),
            pltpu.VMEM((3, 9, 4, 32, SLAB), BF16),
            pltpu.VMEM((9, 3, 32, SLAB), BF16),
            pltpu.VMEM((128, 512), F32),
            pltpu.VMEM((2, 144, 128), BF16),
            pltpu.VMEM((3, 2, 144, 256), BF16),
            pltpu.VMEM((128, 128), F32),
            pltpu.VMEM((128, 128), F32),
            pltpu.VMEM((4, 4, 8, 512), F32),
            pltpu.VMEM((3, 4, 8, 512), F32),
            pltpu.VMEM((4, 32, 128), F32),
            dma((3,)),
            dma((3, 3)),
            dma((3, 7)),
            dma((3, 7)),
            dma((4,)),
            dma((4,)),
            dma((4, 7)),
            dma((4, 7)),
            dma((2, 3, 4)),
            dma((2, 3, 4)),
            dma((3, 4)),
            dma((3, 4)),
            dma((4, 4)),
            dma((4, 4)),
        ],
        compiler_params=pltpu.CompilerParams(
            collective_id=0, has_side_effects=True, vmem_limit_bytes=60 * 2**20
        ),
    )(
        packed,
        slot_blocks.reshape(SLOTS, 128),
        flip_bits,
        ladder_v.reshape(9, 3, 16, 3, 16, 512),
        jnp.asarray(part_matrix()),
    )


def solution(mesh):
    in_specs = (
        P(("row", "col", "depth"), None),
        P(),
        P(("row", "col", "depth")),
        P("depth", None, "col"),
    )
    out_specs = P(("row", "depth"), "col")
    return jax.shard_map(
        per_device, mesh=mesh, in_specs=in_specs, out_specs=out_specs, check_vma=False
    )
```

```python
import jax
import jax.numpy as jnp
import numpy as np
from jax import lax
from jax.experimental import pallas as pl
from jax.experimental.pallas import tpu as pltpu
from jax.sharding import PartitionSpec as P


MESH = pl.DeviceIdType.MESH
TILE = 48 * 48
SLAB = 768
SLOTS = 288
X_ORDER = (0, 1, 3, 2)
STEPS = ((0, 1), (0, 3), (1, 1), (1, 3), (0, 2), (1, 2), (1, 0))
DIAGONAL = (0, 8, 15, 21, 26, 30, 33, 35)
F32 = jnp.float32
BF16 = jnp.bfloat16


def part_matrix():
    a0, b1, b0 = np.meshgrid(np.arange(16), np.arange(3), np.arange(16), indexing="ij")
    out = np.zeros((SLAB, SLAB), np.float32)
    out[(a0 * 48 + b1 * 16 + b0).ravel(), (b1 * 256 + a0 * 16 + b0).ravel()] = 1.0
    return out.astype(jnp.bfloat16)


def dot(a, b):
    return jnp.dot(a, b, preferred_element_type=F32)


def iota(shape, dim):
    return lax.broadcasted_iota(jnp.int32, shape, dim)


def split_ids(ids):
    pair = ((ids >> 2) * 7282) >> 16
    tile = ids - pair * 36
    part = (tile * 57) >> 9
    group = (pair >> 7) * 4 + part
    place = (tile - part * 9) * 32 + ((pair & 127) >> 2)
    return group, place


def loop(count, body):
    def step(i, carry):
        body(i)
        return carry

    lax.fori_loop(0, count, step, 0)


def kernel(
    packed_hbm, ids_hbm, flip_ref, v_hbm, part_hbm, out_ref,
    packed, ids_ref, part, v, nbuf, nrec, sbuf, xbuf, rbuf, ybuf, pmat, dense, late, total, near_lines, lines_of, table, places, cbuf, yrec, mixed,
    load_sem, v_sem, nsend, nrecv, xsend, xrecv, ssend, srecv, zsend, zrecv, fsend, frecv, ysend, yrecv,
):
    r, c, e = lax.axis_index("row"), lax.axis_index("col"), lax.axis_index("depth")
    x, k = r // 2, lax.rem(r, 2)
    here = k * 4 + e
    up, down = lax.rem(c + 1, 4), lax.rem(c + 3, 4)

    load_packed = pltpu.make_async_copy(packed_hbm, packed, load_sem.at[0])
    load_part = pltpu.make_async_copy(part_hbm, part, load_sem.at[1])
    load_ids = pltpu.make_async_copy(ids_hbm, ids_ref, load_sem.at[2])
    load_ids.start()
    load_packed.start()
    load_part.start()

    barrier = pltpu.get_barrier_semaphore()
    near = [(x * 2 + lax.rem(k + k_step, 2), c, lax.rem(e + e_step, 4)) for k_step, e_step in STEPS]
    near += [(lax.rem(x + step, 4) * 2 + k, c, e) for step in (1, 2, 3)]
    near += [(r, up, e), (r, down, e)]
    for device in near:
        pl.semaphore_signal(barrier, inc=1, device_id=device, device_id_type=MESH)

    def load_v(n, b):
        return pltpu.make_async_copy(v_hbm.at[:, n, :, b], v.at[n, :, b], v_sem.at[n, b])

    before = jnp.where(iota((SLOTS, SLOTS), 0) < iota((SLOTS, SLOTS), 1), 1.0, 0.0).astype(BF16)
    flat = (r * 4 + c) * 4 + e
    first = (flat * 9) // 4
    load_ids.wait()
    own = jnp.concatenate([ids_ref[pl.ds(first + i, 1), :] for i in range(3)], axis=1)
    own = pltpu.roll(own, lax.rem(384 - 32 * lax.rem(flat, 4), 384), 1)[:, :SLOTS]
    group, _ = split_ids(own)
    member = jnp.where(iota((32, SLOTS), 0) == group, 1.0, 0.0)
    rank = jnp.sum(member * dot(member.astype(BF16), before), axis=0, keepdims=True)
    target = group * 9 + rank.astype(jnp.int32)
    flips = flip_ref[...].reshape(1, SLOTS) == 1

    swap_in, swap_out = iota((256, 256), 0), iota((256, 256), 1)
    swap = (swap_in & 15) * 16 + (swap_in >> 4) == swap_out
    swap = jnp.where(swap, -1.0, 0.0).astype(BF16)

    def spread(a, rows):
        line, column = iota((8 * rows, 80), 0), iota((8 * rows, 80), 1)
        to, inner = line // rows, line % rows - 9 * a
        hit = (inner >= 0) & (inner < 9) & (column == to * 9 + inner)
        return jnp.where(hit, 1.0, 0.0).astype(BF16)

    spread_near = spread(0, 16)
    spread_far = [spread(a, 32) for a in range(3)]

    load_packed.wait()
    load_part.wait()

    def sort_stage(q, is_near):
        x_to = lax.rem(x + 4 - q, 4)
        line = iota((80, SLOTS), 0)
        hit = (target - x_to * 72 == line) & (line < 72)
        chosen = jnp.where(hit, 1.0, 0.0)
        turned = jnp.sum(jnp.where(flips, chosen, 0.0), axis=1, keepdims=True) > 0.5
        chosen = chosen.astype(BF16)
        parts = []
        for a in range(3):
            rows = dot(chosen, packed[:, a * SLAB:(a + 1) * SLAB]).astype(BF16)
            for b in range(3):
                parts.append(dot(rows, part[:, b * 256:(b + 1) * 256]))
        parts16 = [one.astype(BF16) for one in parts]

        def canon(a, b):
            return jnp.where(turned, dot(parts16[b * 3 + a], swap), parts[a * 3 + b]).astype(BF16)

        if is_near:
            pl.semaphore_wait(barrier, len(near))
            for a in range(3):
                for b in range(3):
                    rows = dot(spread_near, canon(a, b)).astype(BF16)
                    nbuf[a, :, :, b * 256:(b + 1) * 256] = rows.reshape(8, 16, 256)
                if a == 0:
                    send_near(0)
            return
        for b in range(3):
            total = dot(spread_far[0], canon(0, b))
            for a in range(1, 3):
                total = total + dot(spread_far[a], canon(a, b))
            sbuf[q - 1, :, :, b * 256:(b + 1) * 256] = total.astype(BF16).reshape(8, 32, 256)

    def x_copy(q):
        return pltpu.make_async_remote_copy(
            src_ref=sbuf.at[q - 1],
            dst_ref=xbuf.at[q - 1],
            send_sem=xsend.at[q],
            recv_sem=xrecv.at[q],
            device_id=(lax.rem(x + 4 - q, 4) * 2 + k, c, e),
            device_id_type=MESH,
        )

    def near_place(step):
        k_step, e_step = STEPS[step]
        to_k, to_e = lax.rem(k + k_step, 2), lax.rem(e + e_step, 4)
        return to_k * 4 + to_e, (x * 2 + to_k, c, to_e)

    def near_copy(a, step):
        to, device = near_place(step)
        return pltpu.make_async_remote_copy(
            src_ref=nbuf.at[a, to],
            dst_ref=nrec.at[a, here],
            send_sem=nsend.at[a, step],
            recv_sem=nrecv.at[a, step],
            device_id=device,
            device_id_type=MESH,
        )

    def send_near(a):
        for step in range(7):
            near_copy(a, step).start()
        nrec[a, here] = nbuf[a, here]

    def block_copy(q, step):
        to, device = near_place(step)
        return pltpu.make_async_remote_copy(
            src_ref=xbuf.at[q - 1, to],
            dst_ref=rbuf.at[q - 1, here],
            send_sem=ssend.at[q, step],
            recv_sem=srecv.at[q, step],
            device_id=device,
            device_id_type=MESH,
        )

    def pass_blocks(q):
        x_copy(q).wait_recv()
        for step in range(7):
            block_copy(q, step).start()
        rbuf[q - 1, here] = xbuf[q - 1, here]

    def compact(n, h, rows):
        line, column = iota((144, 8 * rows), 0) - 72 * h, iota((144, 8 * rows), 1)
        wanted = (line & 7) * rows + n * 9 + (line >> 3)
        hit = (line >= 0) & (line < 72) & (column == wanted)
        return jnp.where(hit, 1.0, 0.0).astype(BF16)

    def z_copy(at, n, direction):
        return pltpu.make_async_remote_copy(
            src_ref=ybuf.at[0, n, at],
            dst_ref=ybuf.at[3 - 2 * direction, n, at],
            send_sem=zsend.at[direction, n, at],
            recv_sem=zrecv.at[direction, n, at],
            device_id=(r, lax.rem(c + 1 + 2 * direction, 4), e),
            device_id_type=MESH,
        )

    def forward_copy(at, n):
        direction = lax.rem(at + n, 2)
        return pltpu.make_async_remote_copy(
            src_ref=ybuf.at[3 - 2 * direction, n, at],
            dst_ref=ybuf.at[2, n, at],
            send_sem=fsend.at[n, at],
            recv_sem=frecv.at[n, at],
            device_id=(r, lax.rem(c + 1 + 2 * direction, 4), e),
            device_id_type=MESH,
        )

    def send_piece(at, n, rows):
        ybuf[0, n, at] = rows.astype(BF16)
        for direction in range(2):
            z_copy(at, n, direction).start()

    def gather_near(n):
        for step in range(7):
            near_copy(n, step).wait_recv()
        low = nrec[n, :, :, :384].reshape(128, 384)
        high = nrec[n, :, :, 384:].reshape(128, 384)
        send_piece(0, n, dot(near_lines[0], low) + dot(near_lines[1], high))

    def gather_stage(at):
        q = X_ORDER[at]
        for step in range(7):
            block_copy(q, step).wait_recv()

        def piece(n):
            low = rbuf[q - 1, :, :, :384].reshape(256, 384)
            high = rbuf[q - 1, :, :, 384:].reshape(256, 384)
            send_piece(at, n, dot(lines_of[n, 0], low) + dot(lines_of[n, 1], high))

        loop(3, piece)

    def forward_stage(at):
        def piece(n):
            z_copy(at, n, lax.rem(at + n, 2)).wait_recv()
            forward_copy(at, n).start()

        loop(3, piece)

    def wait_other(at, n):
        z_copy(at, n, lax.rem(at + n + 1, 2)).wait_recv()

    def find_places():
        ids = []
        for j in range(4):
            lines = [ids_ref[pl.ds((9 * j) // 4 + i, 32, stride=9), :] for i in range(3)]
            lines = jnp.concatenate(lines, axis=1)
            if j > 0:
                lines = pltpu.roll(lines, 384 - 32 * j, 1)
            ids.append(lines[:, :SLOTS])
        groups, place = split_ids(jnp.concatenate(ids, axis=0))
        mine = groups == r * 4 + e
        nth = dot(jnp.where(mine, 1.0, 0.0).astype(BF16), before)
        nth = jnp.where(mine, nth, -1.0)
        place = place.astype(F32)
        lanes = iota((128, 128), 1)
        found = jnp.full((128, 128), -1.0, F32)
        for n in range(9):
            value = jnp.sum(jnp.where(nth == n, place, 0.0), axis=1, keepdims=True)
            found = jnp.where(lanes == n, value, found)
        table[...] = found
        for j in range(4):
            for c_at in range(4):
                places[pl.ds(c_at * 32 + j, 8, stride=4), :] = table[pl.ds(j * 32 + c_at, 8, stride=4), :]

    scale_tile = iota((SLOTS, 1), 0) // 32 + e * 9
    diagonal = jnp.zeros((SLOTS, 1), jnp.bool_)
    for t in DIAGONAL:
        diagonal = diagonal | (scale_tile == t)
    scale = jnp.where(diagonal, 0.5, 1.0)

    none = jnp.full((8, 128), -1.0, F32)

    def find_order(slot):
        c_at = lax.rem(c + slot, 4)
        lines = [[], []]
        for at, q in enumerate(X_ORDER):
            low = pl.multiple_of(c_at * 32 + lax.rem(x + q, 4) * 8, 8)
            one = places[pl.ds(low, 8), :]
            half = [jnp.broadcast_to(one[:, n:n + 1], (8, 128)) for n in range(9)]
            if at == 2:
                lines = [line + 12 * [none] for line in lines]
            lines[0] += half + [none]
            lines[1] += [none] + half
        for h in range(2):
            wanted = jnp.transpose(jnp.concatenate(lines[h] + 12 * [none], axis=0))[0:1]
            hit = jnp.where(iota((SLOTS, 512), 0).astype(F32) == wanted, scale, 0.0)
            pmat[slot, h] = hit.astype(BF16)

    def place_blocks(slot, n, side, out, at, add=False):
        for h in range(2):
            blocks = [ybuf[slot, n, 2 * side + i, h * 64:h * 64 + 80, :] for i in range(2)]
            order = pmat[slot, h, :, side * 256:side * 256 + 160]
            rows = dot(order, jnp.concatenate(blocks, axis=0)).reshape(9, 32, 384)
            cols = slice(h * 384, (h + 1) * 384)
            if add:
                rows = rows + out[:, at, :, cols].astype(F32)
            out[:, at, :, cols] = rows.astype(BF16)

    def multiply(n, blocks, rows):
        for half in range(2):
            cols = slice(half * 256, half * 256 + 256)
            some = [
                dot(blocks[t].reshape(rows, SLAB), v[n, t, :, :, :, cols].reshape(SLAB, 256))
                for t in range(9)
            ]
            total[128 - rows:, cols] += sum(some[1:], some[0])

    def multiply_early(n):
        for b in range(3):
            load_v(n, b).wait()
        multiply(n, dense.at[n], 128)

    def multiply_late(n):
        wait_other(2, n)
        wait_other(3, n)
        place_blocks(1, n, 1, late, 0)
        place_blocks(3, n, 1, late, 2)
        forward_copy(2, n).wait_recv()
        forward_copy(3, n).wait_recv()
        place_blocks(2, n, 1, late, 1)

        multiply(n, late, 96)

    def sum_copy(slot, step):
        c_at = lax.rem(c + slot, 4)
        to = lax.rem(e + step, 4)
        return pltpu.make_async_remote_copy(
            src_ref=cbuf.at[c_at, to],
            dst_ref=yrec.at[step - 1, c_at],
            send_sem=ysend.at[slot, step],
            recv_sem=yrecv.at[slot, step],
            device_id=(r, c, to),
            device_id_type=MESH,
        )

    def send_sums(slot):
        cbuf[lax.rem(c + slot, 4)] = total[slot * 32:(slot + 1) * 32].reshape(4, 8, 512)
        for step in range(1, 4):
            sum_copy(slot, step).start()

    sort_stage(0, True)
    for n in range(3):
        for b in range(3):
            load_v(n, b).start()

    near_lines[0] = compact(0, 0, 16)
    near_lines[1] = compact(0, 1, 16)
    for n in range(3):
        for h in range(2):
            lines_of[n, h] = compact(n, h, 32)

    def far_stage(i):
        q = 1 + 2 * i - 3 * (i // 2)

        @pl.when(i == 2)
        def _():
            loop(3, gather_near)

        sort_stage(q, False)

        @pl.when(i < 2)
        def _():
            x_copy(q).start()
            for step in range(7):
                near_copy(i, step).wait_send()
            send_near(i + 1)

    loop(3, far_stage)
    find_places()
    pass_blocks(1)
    x_copy(2).start()
    loop(4, find_order)
    forward_stage(0)
    pass_blocks(3)
    gather_stage(1)
    gather_stage(2)
    pass_blocks(2)
    forward_stage(1)
    loop(3, lambda n: place_blocks(0, n, 0, dense.at[n], 0))
    for n in range(3):
        wait_other(0, n)
        wait_other(1, n)
    loop(6, lambda i: place_blocks(1 + 2 * (i // 3), lax.rem(i, 3), 0, dense.at[lax.rem(i, 3)], 1 + 2 * (i // 3)))
    total[...] = jnp.zeros((128, 512), F32)
    forward_stage(2)
    gather_stage(3)
    loop(3, lambda n: place_blocks(0, n, 1, dense.at[n], 0, add=True))
    for n in range(3):
        forward_copy(0, n).wait_recv()
        forward_copy(1, n).wait_recv()
    for n in range(3):
        place_blocks(2, n, 0, dense.at[n], 2)
    for n in range(3):
        multiply_early(n)
        z_copy(3, n, (3 + n) % 2).wait_recv()
        forward_copy(3, n).start()
    send_sums(0)
    for n in range(3):
        multiply_late(n)
    for slot in range(1, 4):
        send_sums(slot)

    for slot in range(4):
        for step in range(1, 4):
            sum_copy(slot, step).wait_recv()
    for c_at in range(4):
        rows = cbuf[c_at, e]
        for step in range(1, 4):
            rows = rows + yrec[step - 1, c_at]
        for n in range(4):
            mixed[n, pl.ds(c_at, 8, stride=4), :] = rows[:, n * 128:(n + 1) * 128]
    for n in range(4):
        out_ref[:, n * 128:(n + 1) * 128] = mixed[n]

    for q in range(4):
        if q > 0:
            x_copy(q).wait_send()
            for step in range(7):
                block_copy(q, step).wait_send()
        else:
            for step in range(7):
                near_copy(2, step).wait_send()
        for n in range(3):
            z_copy(q, n, 0).wait_send()
            z_copy(q, n, 1).wait_send()
            forward_copy(q, n).wait_send()
        for step in range(1, 4):
            sum_copy(q, step).wait_send()


def per_device(packed, slot_blocks, flip_bits, ladder_v):
    any_space = pl.BlockSpec(memory_space=pl.ANY)
    in_vmem = pl.BlockSpec(memory_space=pltpu.VMEM)
    dma = pltpu.SemaphoreType.DMA
    return pl.pallas_call(
        kernel,
        out_shape=jax.ShapeDtypeStruct((32, 512), F32),
        in_specs=[any_space, any_space, in_vmem, any_space, any_space],
        out_specs=in_vmem,
        scratch_shapes=[
            pltpu.VMEM((SLOTS, TILE), BF16),
            pltpu.VMEM((SLOTS, 128), jnp.int32),
            pltpu.VMEM((SLAB, SLAB), BF16),
            pltpu.VMEM((3, 9, 3, 16, 16, 512), BF16),
            pltpu.VMEM((3, 8, 16, SLAB), BF16),
            pltpu.VMEM((3, 8, 16, SLAB), BF16),
            pltpu.VMEM((3, 8, 32, SLAB), BF16),
            pltpu.VMEM((3, 8, 32, SLAB), BF16),
            pltpu.VMEM((3, 8, 32, SLAB), BF16),
            pltpu.VMEM((4, 3, 4, 144, 384), BF16),
            pltpu.VMEM((4, 2, SLOTS, 512), BF16),
            pltpu.VMEM((3, 9, 4, 32, SLAB), BF16),
            pltpu.VMEM((9, 3, 32, SLAB), BF16),
            pltpu.VMEM((128, 512), F32),
            pltpu.VMEM((2, 144, 128), BF16),
            pltpu.VMEM((3, 2, 144, 256), BF16),
            pltpu.VMEM((128, 128), F32),
            pltpu.VMEM((128, 128), F32),
            pltpu.VMEM((4, 4, 8, 512), F32),
            pltpu.VMEM((3, 4, 8, 512), F32),
            pltpu.VMEM((4, 32, 128), F32),
            dma((3,)),
            dma((3, 3)),
            dma((3, 7)),
            dma((3, 7)),
            dma((4,)),
            dma((4,)),
            dma((4, 7)),
            dma((4, 7)),
            dma((2, 3, 4)),
            dma((2, 3, 4)),
            dma((3, 4)),
            dma((3, 4)),
            dma((4, 4)),
            dma((4, 4)),
        ],
        compiler_params=pltpu.CompilerParams(
            collective_id=0, has_side_effects=True, vmem_limit_bytes=60 * 2**20
        ),
    )(
        packed,
        slot_blocks.reshape(SLOTS, 128),
        flip_bits,
        ladder_v.reshape(9, 3, 16, 3, 16, 512),
        jnp.asarray(part_matrix()),
    )


def solution(mesh):
    in_specs = (
        P(("row", "col", "depth"), None),
        P(),
        P(("row", "col", "depth")),
        P("depth", None, "col"),
    )
    out_specs = P(("row", "depth"), "col")
    return jax.shard_map(
        per_device, mesh=mesh, in_specs=in_specs, out_specs=out_specs, check_vma=False
    )
```
